256 devices in a mesh: section: 8 (over z), expert: 32 (over x, y, core).
Axes of the slice: x: 4, y: 4, z: 8, core: 2. Of those that a mesh axis runs over, the one named last changes fastest.
Arguments:
- tokens_a: bfloat16 [8, 4096, 2048], P('section', 'expert'), may hold values from -6 to 6
- routes_a: int32 [8, 4096, 8], P('section', 'expert'), may hold values from 0 to 31, all different within a row; in each aligned block of 128 rows (0 to 127, 128 to 255, ..., all dimensions but the last counted through in order) at most 40 rows name the same one
- gates_a: float32 [8, 4096, 8], P('section', 'expert'), may hold values from 0.05 to 0.5
- w_gate: bfloat16 [8, 32, 2048, 768], P('section', 'expert'), may hold values from -0.125 to 0.125
- w_up: bfloat16 [8, 32, 2048, 768], P('section', 'expert'), may hold values from -0.125 to 0.125
- w_down: bfloat16 [8, 32, 768, 2048], P('section', 'expert'), may hold values from -0.21875 to 0.21875
Outputs:
- next_input: bfloat16 [8, 4096, 2048], P('section', 'expert')
The draws below stay inside these ranges and needn't reach their ends.
Inputs may be any that keep to these rules, and one draw needn't show every extreme that they name: `routes_a`: each row names 8 different experts; in each aligned block of 128 rows (the tokens of one device) no expert is named by more than 40 rows, a bound that some block reaches.
All inputs are finite; a program needn't handle non-finite values.
Results may differ from the reference program's by a relative error of at most 0.0075.
Values may be sent and summed in bfloat16 or wider, within the bound.
No kernel may reach another device: no remote copies, remote signals or barrier semaphores. Data moves between devices by JAX's collectives and lax.ppermute only.
A program may use at most 128 MiB of HBM per device.

```python
import math
import jax
import jax.numpy as jnp
import numpy as np
from jax import lax

D = 2048
FF = 768
EXPERTS = 32
TOP = 8
TOK_DEV = 128
CAP = 40
TOKENS = 4096
SECTIONS = 8
N_EXPERT = 32


def steps_of(rng, extent, cuts, low, top_value):
    level = 1.0
    for axis_at, parts in cuts:
        steps = jax.random.uniform(jax.random.fold_in(jax.random.fold_in(rng, 6), axis_at), (parts,), jnp.float32, low / len(cuts), top_value / len(cuts))
        level = level * jnp.repeat(jnp.exp(steps), extent[axis_at] // parts).reshape((-1,) + (1,) * (len(extent) - 1 - axis_at))
    return level


def assign_block(rng, own, number, rows, count, top, most, lean):
    sequence = jax.random.permutation(rng, count)
    packed, usual = shares(count, rows * top, most, lean, True), shares(count, rows * top, most, lean, False)
    places = jnp.arange(count)

    def named(sizes, offset_by):
        used = int((sizes > 0).sum())
        fixed = max(1, used // 4)
        passed = fixed + (places - fixed + offset_by * (used - fixed)) % max(1, count - fixed)
        return jnp.zeros((count,), jnp.int32).at[sequence[jnp.where(places < fixed, places, passed)]].set(jnp.asarray(sizes, jnp.int32))

    sizes = jnp.where(number % 4 == 0, named(packed, number // 4), named(usual, number - number // 4 - 1))
    mixed = jax.random.permutation(jax.random.fold_in(own, 3), count)
    source_of, sink = mixed[0:count // 2 * 2:2], mixed[1:count // 2 * 2:2]
    room = jnp.minimum(sizes[source_of] - 1, most - sizes[sink]) // 2
    room = jnp.where((source_of == sequence[0]) | (sink == sequence[0]) | (sizes[sink] == 0), 0, jnp.maximum(room, 0))
    passed = jax.random.randint(jax.random.fold_in(own, 4), (count // 2,), 0, 1 << 20) % (room + 1)
    sizes = sizes.at[source_of].add(-passed).at[sink].add(passed)
    items = jnp.searchsorted(jnp.cumsum(sizes), jnp.arange(rows * top), side="right").astype(jnp.int32)
    grid = items.reshape(top, rows).T
    grid = grid[jax.random.permutation(jax.random.fold_in(own, 1), rows)]
    offset_by = jax.random.randint(jax.random.fold_in(own, 2), (rows, 1), 0, top)
    return jnp.take_along_axis(grid, (jnp.arange(top)[None, :] + offset_by) % top, axis=1)


def shares(count, total, limit, skew, full):
    weights = [(1 << 20) // math.isqrt(standing ** skew) + 1 for standing in range(1, count + 1)]
    largest = limit if full else min(limit, max(-(-total // count), total * weights[0] // sum(weights)))
    least = 1 if total - largest >= count - 1 else 0
    counts, spare = [largest] + [least] * (count - 1), total - largest - least * (count - 1)
    while spare > 0:
        movable = [i for i in range(1, count) if counts[i] < largest] or [i for i in range(1, count) if counts[i] < limit]
        mass, left = sum([weights[i] for i in movable]), spare
        for i in movable:
            more = min(limit - counts[i], max(1, left * weights[i] // mass), spare)
            counts[i] = counts[i] + more
            spare = spare - more
    return np.array(counts)


def scatter_about(key, extent, width, bound, pieces=(), kind=jnp.bfloat16):
    values = width * jax.random.normal(key, extent, jnp.float32)
    if pieces:
        values = values * steps_of(key, extent, pieces, -0.22, 0.18)
    return jnp.clip(values, -bound, bound).astype(kind)


def setup_inputs(seed: int = 0) -> dict:
    keys = jax.random.split(jax.random.key(seed), 7)
    tokens_a = scatter_about(keys[0], (SECTIONS, TOKENS, D), 1.0, 6.0, ((0, 8), (1, 32)))
    routes_a_keys = jax.random.split(jax.random.fold_in(keys[1], 1), SECTIONS * TOKENS // TOK_DEV)
    routes_a_turns = jax.random.permutation(jax.random.fold_in(keys[1], 3), SECTIONS * TOKENS // TOK_DEV)
    routes_a = jax.vmap(lambda own, number: assign_block(jax.random.fold_in(keys[1], 2), own, number, TOK_DEV, EXPERTS, TOP, CAP, 2))(routes_a_keys, routes_a_turns).reshape((SECTIONS, TOKENS, TOP))
    gates_a = jnp.clip(jnp.exp(math.log(0.5) - 2.3025851 * jax.random.uniform(keys[2], (SECTIONS, TOKENS, TOP), jnp.float32) ** steps_of(keys[2], (SECTIONS, TOKENS, TOP), ((0, 8), (1, 32)), -0.2, 0.2)), 0.05, 0.5)
    w_gate = scatter_about(keys[3], (SECTIONS, EXPERTS, D, FF), D ** -0.5, 0.125, ((0, 8), (1, 32)))
    w_up = scatter_about(keys[4], (SECTIONS, EXPERTS, D, FF), D ** -0.5, 0.125, ((0, 8), (1, 32)))
    w_down = scatter_about(keys[5], (SECTIONS, EXPERTS, FF, D), FF ** -0.5, 0.21875, ((0, 8), (1, 32)))
    return {"tokens_a": tokens_a, "routes_a": routes_a, "gates_a": gates_a, "w_gate": w_gate, "w_up": w_up, "w_down": w_down}


def slot_columns(routes):
    blocks = routes.reshape(N_EXPERT, TOK_DEV * TOP)
    onehot = (blocks[:, :, None] == jnp.arange(EXPERTS, dtype=jnp.int32)[None, None, :]).astype(jnp.int32)
    before = jnp.cumsum(onehot, axis=1) - onehot
    slot = jnp.sum(before * onehot, axis=2).reshape(TOKENS, TOP)
    source = (jnp.arange(TOKENS, dtype=jnp.int32) // TOK_DEV) * CAP
    return (source[:, None] + slot).astype(jnp.int32)


def to_slots(values, routes, columns):
    buffer = jnp.zeros((EXPERTS, N_EXPERT * CAP, D), jnp.bfloat16)
    repeated = jnp.repeat(values, TOP, axis=0)
    return buffer.at[routes.reshape(-1), columns.reshape(-1)].set(repeated)


def from_slots(results, routes, columns, gates):
    picked = results[routes, columns].astype(jnp.float32)
    return jnp.sum(gates[:, :, None] * picked, axis=1)


def section_step(inputs):
    tokens_a, routes_a, gates_a, w_gate, w_up, w_down = inputs
    wg = w_gate.astype(jnp.float32)
    wu = w_up.astype(jnp.float32)
    wd = w_down.astype(jnp.float32)
    columns_a = slot_columns(routes_a)
    rows_a = to_slots(tokens_a, routes_a, columns_a).astype(jnp.float32)
    pre_g = jnp.einsum('erd,edf->erf', rows_a, wg)
    pre_u = jnp.einsum('erd,edf->erf', rows_a, wu)
    hidden = (jax.nn.silu(pre_g) * pre_u).astype(jnp.bfloat16)
    expert_out = jnp.einsum('erf,efd->erd', hidden.astype(jnp.float32), wd).astype(jnp.bfloat16)
    layer_a = (tokens_a.astype(jnp.float32) + from_slots(expert_out, routes_a, columns_a, gates_a)).astype(jnp.bfloat16)
    return layer_a


def reference(tokens_a, routes_a, gates_a, w_gate, w_up, w_down):
    layer_a = lax.map(section_step, (tokens_a, routes_a, gates_a, w_gate, w_up, w_down))
    return jnp.roll(layer_a, 1, axis=0)
```

```python
import functools

import jax
import jax.numpy as jnp
from jax import lax
from jax.experimental import pallas as pl
from jax.experimental.pallas import tpu as pltpu
from jax.sharding import PartitionSpec as P

EXPERTS = 32
CAP = 40
SIDE = 4
TOK = 128
TOP = 8
D = 2048
FF = 768
HALF = 1024
TILE = 256
PAIR = 2 * CAP
TARGETS = [(d, flip) for d in (1, 3, 2, 0) for flip in (0, 1)]


def place(x, y, core):
    return ((x % SIDE) * SIDE + y % SIDE) * 2 + core % 2


def routes_of(step):
    return [
        (place(x, y, core), place(*step(x, y, core)))
        for x in range(SIDE)
        for y in range(SIDE)
        for core in range(2)
    ]


def gather_route(d):
    return routes_of(lambda x, y, core: (x + d, y, core) if core == 0 else (x, y + d, core))


def slot_route(d, flip):
    return routes_of(
        lambda x, y, core: (x, y + d, core + flip) if core == 0 else (x + d, y, core + flip)
    )


def back(route):
    return [(b, a) for a, b in route]


def target_experts():
    me = lax.axis_index("expert")
    x, y, core = me // (2 * SIDE), (me // 2) % SIDE, me % 2
    ids = [
        jnp.where(core == 0, place(x, y + d, core + flip), place(x + d, y, core + flip))
        for d, flip in TARGETS
    ]
    return jnp.stack(ids).astype(jnp.int32)


def tables_kernel(ids_ref, *refs):
    named_refs, spread, gather, slots = refs[0:4], refs[4], refs[5], refs[6]
    expert = lax.broadcasted_iota(jnp.int32, (EXPERTS, TOK), 0).astype(jnp.float32)
    earlier = lax.broadcasted_iota(jnp.int32, (TOK, TOK), 0) < lax.broadcasted_iota(
        jnp.int32, (TOK, TOK), 1
    )
    earlier = jnp.where(earlier, 1.0, 0.0).astype(jnp.bfloat16)
    for j, block in enumerate(named_refs):
        named = jnp.zeros((EXPERTS, TOK), jnp.float32)
        gate = jnp.zeros((EXPERTS, TOK), jnp.float32)
        for k in range(TOP):
            hit = expert == block[k : k + 1, :]
            named = named + jnp.where(hit, 1.0, 0.0)
            gate = gate + jnp.where(hit, block[TOP + k : TOP + k + 1, :], 0.0)
        before = jnp.dot(named.astype(jnp.bfloat16), earlier, preferred_element_type=jnp.float32)
        slots[j, 0:EXPERTS, :] = jnp.where(named > 0.0, before, -1.0)
        slots[j, EXPERTS : 2 * EXPERTS, :] = gate
    slot = lax.broadcasted_iota(jnp.int32, (CAP, TOK), 0).astype(jnp.float32)
    empty = jnp.zeros((CAP, TOK), jnp.float32)
    for pair in range(2):
        whole = []
        for i in range(len(TARGETS)):
            e = ids_ref[i]
            halves = []
            for j in (2 * pair, 2 * pair + 1):
                hit = slot == slots[j, pl.ds(e, 1), :]
                spread[j, i * CAP : (i + 1) * CAP, :] = jnp.where(hit, 1.0, 0.0)
                halves.append(jnp.where(hit, slots[j, pl.ds(e + EXPERTS, 1), :], 0.0))
            whole.append(jnp.concatenate([halves[0], empty], axis=1))
            whole.append(jnp.concatenate([empty, halves[1]], axis=1))
        gather[pair] = jnp.concatenate(whole, axis=0).T.astype(jnp.bfloat16)


VMEM = pl.BlockSpec(memory_space=pltpu.VMEM)
SMEM = pl.BlockSpec(memory_space=pltpu.SMEM)


def params(mib):
    return pltpu.CompilerParams(vmem_limit_bytes=mib << 20)


def slot_tables(ids, named):
    return pl.pallas_call(
        tables_kernel,
        out_shape=[
            jax.ShapeDtypeStruct((4, len(TARGETS) * CAP, TOK), jnp.float32),
            jax.ShapeDtypeStruct((2, 2 * TOK, len(TARGETS) * PAIR), jnp.bfloat16),
        ],
        in_specs=[SMEM] + [VMEM] * 4,
        out_specs=[VMEM] * 2,
        scratch_shapes=[pltpu.VMEM((4, 2 * EXPERTS, TOK), jnp.float32)],
        compiler_params=params(16),
        cost_estimate=pl.CostEstimate(flops=1 << 30, bytes_accessed=0, transcendentals=0),
        name="tables",
    )(ids, *named)


def fill_kernel(first, spread, *refs):
    tokens, outs = refs[0:4], refs[4:]
    rows = pl.ds(first * CAP, len(outs) * CAP)
    for t in range(D // TILE):
        cut = pl.ds(t * TILE, TILE)
        made = [
            jnp.dot(
                spread[j, rows, :].astype(jnp.bfloat16),
                tokens[j][:, cut],
                preferred_element_type=jnp.float32,
            )
            for j in range(4)
        ]
        for i, out in enumerate(outs):
            out[:, cut] = jnp.concatenate(
                [m[i * CAP : (i + 1) * CAP] for m in made], axis=0
            ).astype(jnp.bfloat16)


def fill_slots(spread, tokens, first, count):
    return pl.pallas_call(
        functools.partial(fill_kernel, first),
        out_shape=[jax.ShapeDtypeStruct((2 * PAIR, D), jnp.bfloat16)] * count,
        in_specs=[VMEM] * 5,
        out_specs=[VMEM] * count,
        compiler_params=params(16),
        cost_estimate=pl.CostEstimate(flops=1 << 30, bytes_accessed=0, transcendentals=0),
        name="fill",
    )(spread, *tokens)


def combine_kernel(half, *refs):
    weights, rows, outs, gathered = refs[0], refs[1:9], refs[9:13], refs[13]
    for pair in range(2):
        for t in range(HALF // (2 * TILE)):
            cut = pl.ds(t * 2 * TILE, 2 * TILE)
            source = pl.ds(half * HALF + t * 2 * TILE, 2 * TILE)
            for i in range(len(TARGETS)):
                gathered[i * PAIR : (i + 1) * PAIR, :] = rows[i][
                    pair * PAIR : (pair + 1) * PAIR, source
                ]
            mixed = jnp.dot(weights[pair], gathered[...], preferred_element_type=jnp.float32)
            outs[2 * pair][:, cut] = mixed[0:TOK].astype(jnp.bfloat16)
            outs[2 * pair + 1][:, cut] = mixed[TOK : 2 * TOK].astype(jnp.bfloat16)


def combine(weights, rows, half):
    return pl.pallas_call(
        functools.partial(combine_kernel, half),
        out_shape=[jax.ShapeDtypeStruct((TOK, HALF), jnp.bfloat16)] * 4,
        in_specs=[VMEM] * 9,
        out_specs=[VMEM] * 4,
        scratch_shapes=[pltpu.VMEM((len(TARGETS) * PAIR, 2 * TILE), jnp.bfloat16)],
        compiler_params=params(16),
        cost_estimate=pl.CostEstimate(flops=1 << 31, bytes_accessed=0, transcendentals=0),
        name="combine",
    )(weights, *rows)


def expert_kernel(*refs):
    n = (len(refs) - 4) // 2
    rows, (w_gate, w_up, w_down), outs, hidden = refs[:n], refs[n : n + 3], refs[n + 3 : -1], refs[-1]
    for f in range(FF // TILE):
        cut = pl.ds(f * TILE, TILE)
        block = jnp.concatenate([r[...] for r in rows], axis=0)
        pre_g = jnp.dot(block, w_gate[:, cut], preferred_element_type=jnp.float32)
        pre_u = jnp.dot(block, w_up[:, cut], preferred_element_type=jnp.float32)
        hidden[:, cut] = (pre_g / (1.0 + jnp.exp(-pre_g)) * pre_u).astype(jnp.bfloat16)
    for t in range(D // (2 * TILE)):
        cut = pl.ds(t * 2 * TILE, 2 * TILE)
        done = jnp.dot(hidden[...], w_down[:, cut], preferred_element_type=jnp.float32)
        at = 0
        for out in outs:
            out[:, cut] = done[at : at + out.shape[0]].astype(jnp.bfloat16)
            at += out.shape[0]


def expert_forward(rows, w_gate, w_up, w_down):
    total = sum(r.shape[0] for r in rows)
    return pl.pallas_call(
        expert_kernel,
        out_shape=[jax.ShapeDtypeStruct(r.shape, jnp.bfloat16) for r in rows],
        in_specs=[VMEM] * (len(rows) + 3),
        out_specs=[VMEM] * len(rows),
        scratch_shapes=[pltpu.VMEM((total, FF), jnp.bfloat16)],
        compiler_params=params(16),
        cost_estimate=pl.CostEstimate(flops=6 * total * D * FF, bytes_accessed=0, transcendentals=0),
        name="expert",
    )(*rows, w_gate, w_up, w_down)


def on_device(tokens_a, routes_a, gates_a, w_gate, w_up, w_down):
    own = tokens_a[0]
    send = functools.partial(lax.ppermute, axis_name="expert")
    steps = (1, 3, 2)
    named = jnp.concatenate([routes_a[0].astype(jnp.float32).T, gates_a[0].T])
    named = [named] + [send(named, perm=gather_route(d)) for d in steps]
    tokens = [own] + [send(own, perm=gather_route(d)) for d in steps]
    spread, weights = slot_tables(target_experts(), named)
    filled = fill_slots(spread, tokens, 0, 4) + fill_slots(spread, tokens, 4, 4)
    results = [None] * len(TARGETS)
    for n in (6, 0, 2, 4):
        arrived = [
            filled[i] if TARGETS[i] == (0, 0) else send(filled[i], perm=slot_route(*TARGETS[i]))
            for i in (n, n + 1)
        ]
        done = expert_forward(arrived, w_gate[0, 0], w_up[0, 0], w_down[0, 0])
        for i, out in zip((n, n + 1), done):
            results[i] = (
                out if TARGETS[i] == (0, 0) else send(out, perm=back(slot_route(*TARGETS[i])))
            )
    count = lax.axis_size("section")
    onward = [((i - 1) % count, i) for i in range(count)]
    moved = []
    for half in range(2):
        partial = combine(weights, results, half)
        mixed = own[:, half * HALF : (half + 1) * HALF].astype(jnp.float32)
        mixed = mixed + partial[0].astype(jnp.float32)
        for d, block in zip(steps, partial[1:]):
            mixed = mixed + send(block, perm=back(gather_route(d))).astype(jnp.float32)
        moved.append(lax.ppermute(mixed.astype(jnp.bfloat16), "section", onward))
    return jnp.concatenate(moved, axis=1)[None]


def solution(mesh):
    in_specs = (
        P("section", "expert", None),
        P("section", "expert", None),
        P("section", "expert", None),
        P("section", "expert", None, None),
        P("section", "expert", None, None),
        P("section", "expert", None, None),
    )
    out_specs = P("section", "expert", None)
    return jax.shard_map(
        on_device, mesh=mesh, in_specs=in_specs, out_specs=out_specs, check_vma=False
    )
```

```python
import functools

import jax
import jax.numpy as jnp
from jax import lax
from jax.experimental import pallas as pl
from jax.experimental.pallas import tpu as pltpu
from jax.sharding import PartitionSpec as P

EXPERTS = 32
CAP = 40
SIDE = 4
TOK = 128
TOP = 8
D = 2048
FF = 768
HALF = 1024
TILE = 256
PAIR = 2 * CAP
STEPS = (1, 3, 2)
TARGETS = [(d, flip) for d in (0, 1, 3, 2) for flip in (0, 1)]
VMEM = pl.BlockSpec(memory_space=pltpu.VMEM)
SMEM = pl.BlockSpec(memory_space=pltpu.SMEM)
ANY = pl.BlockSpec(memory_space=pl.ANY)


def place(x, y, core):
    return ((x % SIDE) * SIDE + y % SIDE) * 2 + core % 2


def routes_of(step):
    return [
        (place(x, y, core), place(*step(x, y, core)))
        for x in range(SIDE)
        for y in range(SIDE)
        for core in range(2)
    ]


def gather_route(d):
    return routes_of(lambda x, y, core: (x + d, y, core) if core == 0 else (x, y + d, core))


def slot_route(d, flip):
    return routes_of(
        lambda x, y, core: (x, y + d, core + flip) if core == 0 else (x + d, y, core + flip)
    )


def back(route):
    return [(b, a) for a, b in route]


def target_experts():
    me = lax.axis_index("expert")
    x, y, core = me // (2 * SIDE), (me // 2) % SIDE, me % 2
    ids = [
        jnp.where(core == 0, place(x, y + d, core + flip), place(x + d, y, core + flip))
        for d, flip in TARGETS
    ]
    return jnp.stack(ids).astype(jnp.int32)


def call(kernel, name, out_shape, args, scratch=(), after=(), flops=1 << 20):
    one = not isinstance(out_shape, list)
    count = 1 if one else len(out_shape)
    n = len(args)

    def body(*refs):
        kernel(*refs[:n], *refs[n + len(after) :])

    return pl.pallas_call(
        body,
        out_shape=out_shape,
        in_specs=[SMEM if a.dtype == jnp.int32 and a.ndim == 1 else VMEM for a in args]
        + [ANY] * len(after),
        out_specs=VMEM if one else [VMEM] * count,
        scratch_shapes=list(scratch),
        compiler_params=pltpu.CompilerParams(vmem_limit_bytes=16 << 20),
        cost_estimate=pl.CostEstimate(flops=flops, bytes_accessed=0, transcendentals=0),
        name=name,
    )(*args, *after)


def bf16(*shape):
    return jax.ShapeDtypeStruct(shape, jnp.bfloat16)


def f32(*shape):
    return jax.ShapeDtypeStruct(shape, jnp.float32)


def pack_kernel(own, routes, gates, packed, named, gated, sems):
    copies = [
        pltpu.make_async_copy(routes, named, sems.at[0]),
        pltpu.make_async_copy(gates, gated, sems.at[1]),
        pltpu.make_async_copy(own, packed.at[:, 0:D], sems.at[2]),
    ]
    for copy in copies:
        copy.start()
    packed[2 * TOP :, D:] = jnp.zeros((TOK - 2 * TOP, TOK), jnp.bfloat16)
    copies[0].wait()
    copies[1].wait()
    both = jnp.concatenate([named[...].astype(jnp.float32), gated[...]], axis=0)
    packed[0 : 2 * TOP, D:] = both.astype(jnp.bfloat16)
    copies[2].wait()


def slots_kernel(ids, *refs):
    blocks, (spread, slots) = refs[0:4], refs[4:]
    expert = lax.broadcasted_iota(jnp.int32, (EXPERTS, TOK), 0).astype(jnp.float32)
    earlier = lax.broadcasted_iota(jnp.int32, (TOK, TOK), 0) < lax.broadcasted_iota(
        jnp.int32, (TOK, TOK), 1
    )
    earlier = jnp.where(earlier, 1.0, 0.0).astype(jnp.bfloat16)
    slot = lax.broadcasted_iota(jnp.int32, (CAP, TOK), 0).astype(jnp.float32)
    for j in range(4):
        block = blocks[j][0 : 2 * TOP, D:].astype(jnp.float32)
        named = jnp.zeros((EXPERTS, TOK), jnp.float32)
        gate = jnp.zeros((EXPERTS, TOK), jnp.float32)
        for k in range(TOP):
            hit = expert == block[k : k + 1, :]
            named = named + jnp.where(hit, 1.0, 0.0)
            gate = gate + jnp.where(hit, block[TOP + k : TOP + k + 1, :], 0.0)
        before = jnp.dot(named.astype(jnp.bfloat16), earlier, preferred_element_type=jnp.float32)
        slots[j, 0:EXPERTS, :] = jnp.where(named > 0.0, before, -1.0)
        slots[j, EXPERTS : 2 * EXPERTS, :] = gate
        for i in range(len(TARGETS)):
            hit = slot == slots[j, pl.ds(ids[i], 1), :]
            spread[j, i * CAP : (i + 1) * CAP, :] = jnp.where(hit, 1.0, 0.0)


def weights_kernel(ids, slots, weights):
    slot = lax.broadcasted_iota(jnp.int32, (CAP, TOK), 0).astype(jnp.float32)
    empty = jnp.zeros((CAP, TOK), jnp.float32)
    for pair in range(2):
        whole = []
        for i in range(len(TARGETS)):
            halves = []
            for j in (2 * pair, 2 * pair + 1):
                hit = slot == slots[j, pl.ds(ids[i], 1), :]
                halves.append(jnp.where(hit, slots[j, pl.ds(ids[i] + EXPERTS, 1), :], 0.0))
            whole.append(jnp.concatenate([halves[0], empty], axis=1))
            whole.append(jnp.concatenate([empty, halves[1]], axis=1))
        weights[pair] = jnp.concatenate(whole, axis=0).T.astype(jnp.bfloat16)


def fill_kernel(first, spread, *refs):
    tokens, outs = refs[0:4], refs[4:]
    rows = pl.ds(first * CAP, len(outs) * CAP)
    for t in range(D // TILE):
        cut = pl.ds(t * TILE, TILE)
        made = [
            jnp.dot(
                spread[j, rows, :].astype(jnp.bfloat16),
                tokens[j][:, cut],
                preferred_element_type=jnp.float32,
            )
            for j in range(4)
        ]
        for i, out in enumerate(outs):
            out[:, cut] = jnp.concatenate(
                [m[i * CAP : (i + 1) * CAP] for m in made], axis=0
            ).astype(jnp.bfloat16)


def fill_slots(spread, tokens, first, count, after=()):
    kernel = functools.partial(fill_kernel, first)
    return call(kernel, "fill", [bf16(2 * PAIR, D)] * count, (spread, *tokens), after=after)


def expert_kernel(*refs):
    n = (len(refs) - 4) // 2
    rows, (w_gate, w_up, w_down), outs, hidden = refs[:n], refs[n : n + 3], refs[n + 3 : -1], refs[-1]
    for f in range(FF // TILE):
        cut = pl.ds(f * TILE, TILE)
        block = jnp.concatenate([r[...] for r in rows], axis=0)
        pre_g = jnp.dot(block, w_gate[:, cut], preferred_element_type=jnp.float32)
        pre_u = jnp.dot(block, w_up[:, cut], preferred_element_type=jnp.float32)
        hidden[:, cut] = (pre_g / (1.0 + jnp.exp(-pre_g)) * pre_u).astype(jnp.bfloat16)
    for t in range(D // (2 * TILE)):
        cut = pl.ds(t * 2 * TILE, 2 * TILE)
        done = jnp.dot(hidden[...], w_down[:, cut], preferred_element_type=jnp.float32)
        at = 0
        for out in outs:
            out[:, cut] = done[at : at + out.shape[0]].astype(jnp.bfloat16)
            at += out.shape[0]


def expert_forward(rows, weights, after=()):
    total = sum(r.shape[0] for r in rows)
    scratch = [pltpu.VMEM((total, FF), jnp.bfloat16)]
    outs = [bf16(*r.shape) for r in rows]
    flops = 6 * total * D * FF
    return call(expert_kernel, "expert", outs, (*rows, *weights), scratch, after, flops)


def combine_kernel(half, *refs):
    weights, rows, outs, gathered = refs[0], refs[1:9], refs[9:13], refs[13]
    for pair in range(2):
        for t in range(HALF // (2 * TILE)):
            cut = pl.ds(t * 2 * TILE, 2 * TILE)
            source = pl.ds(half * HALF + t * 2 * TILE, 2 * TILE)
            for i in range(len(TARGETS)):
                gathered[i * PAIR : (i + 1) * PAIR, :] = rows[i][
                    pair * PAIR : (pair + 1) * PAIR, source
                ]
            mixed = jnp.dot(weights[pair], gathered[...], preferred_element_type=jnp.float32)
            outs[2 * pair][:, cut] = mixed[0:TOK].astype(jnp.bfloat16)
            outs[2 * pair + 1][:, cut] = mixed[TOK : 2 * TOK].astype(jnp.bfloat16)


def combine(weights, rows, half, after=()):
    kernel = functools.partial(combine_kernel, half)
    scratch = [pltpu.VMEM((len(TARGETS) * PAIR, 2 * TILE), jnp.bfloat16)]
    return call(kernel, "combine", [bf16(TOK, HALF)] * 4, (weights, *rows), scratch, after)


def finish_kernel(half, own, *refs):
    blocks, out = refs[:4], refs[4]
    mixed = own[:, half * HALF : (half + 1) * HALF].astype(jnp.float32)
    for block in blocks:
        mixed = mixed + block[...].astype(jnp.float32)
    out[...] = mixed.astype(jnp.bfloat16)


def on_device(tokens_a, routes_a, gates_a, w_gate, w_up, w_down):
    own = tokens_a[0]
    expert = (w_gate[0, 0], w_up[0, 0], w_down[0, 0])
    ids = target_experts()

    def send(block, route):
        return lax.ppermute(block, "expert", route)

    packed = pl.pallas_call(
        pack_kernel,
        out_shape=bf16(TOK, D + TOK),
        in_specs=[ANY] * 3,
        out_specs=VMEM,
        scratch_shapes=[
            pltpu.VMEM((TOP, TOK), jnp.int32),
            pltpu.VMEM((TOP, TOK), jnp.float32),
            pltpu.SemaphoreType.DMA((3,)),
        ],
        compiler_params=pltpu.CompilerParams(vmem_limit_bytes=16 << 20),
        name="pack",
    )(own, routes_a[0].T, gates_a[0].T)
    tokens = [packed] + [send(packed, gather_route(d)) for d in STEPS]
    spread, slots = call(
        slots_kernel,
        "slots",
        [f32(4, len(TARGETS) * CAP, TOK), f32(4, 2 * EXPERTS, TOK)],
        (ids, *tokens),
    )

    def out(i, block):
        return send(block, slot_route(*TARGETS[i]))

    def home(i, block):
        return send(block, back(slot_route(*TARGETS[i])))

    results = [None] * len(TARGETS)
    near_rows = fill_slots(spread, tokens, 2, 4)
    near = [out(i + 2, block) for i, block in enumerate(near_rows)]
    far = fill_slots(spread, tokens, 6, 2, after=(near_rows[0],))
    far = [out(i + 6, block) for i, block in enumerate(far)]
    here = list(fill_slots(spread, tokens, 0, 2))
    here[1] = out(1, here[1])
    weights = call(weights_kernel, "weights", bf16(2, 2 * TOK, len(TARGETS) * PAIR), (ids, slots))
    after = ()
    for n, rows in ((2, near[0:2]), (4, near[2:4]), (6, far), (0, here)):
        done = expert_forward(rows, expert, after)
        results[n : n + 2] = [
            block if n + i == 0 else home(n + i, block) for i, block in enumerate(done)
        ]
    count = lax.axis_size("section")
    onward = [((i - 1) % count, i) for i in range(count)]
    moved, after = [], ()
    for half in range(2):
        partial = combine(weights, results, half, after)
        after = (partial[0],)
        arrived = [send(block, back(gather_route(d))) for d, block in zip(STEPS, partial[1:])]
        layer_a = call(
            functools.partial(finish_kernel, half),
            "finish",
            bf16(TOK, HALF),
            (packed, partial[0], *arrived),
        )
        moved.append(lax.ppermute(layer_a, "section", onward))
    return jnp.concatenate(moved, axis=1)[None]


def solution(mesh):
    in_specs = (
        P("section", "expert", None),
        P("section", "expert", None),
        P("section", "expert", None),
        P("section", "expert", None, None),
        P("section", "expert", None, None),
        P("section", "expert", None, None),
    )
    out_specs = P("section", "expert", None)
    return jax.shard_map(
        on_device, mesh=mesh, in_specs=in_specs, out_specs=out_specs, check_vma=False
    )
```

```python
import functools

import jax
import jax.numpy as jnp
from jax import lax
from jax.experimental import pallas as pl
from jax.experimental.pallas import tpu as pltpu
from jax.sharding import PartitionSpec as P

EXPERTS = 32
CAP = 40
SIDE = 4
TOK = 128
TOP = 8
D = 2048
FF = 768
PARTS = (0, 1024, D)
TILE = 256
PAIR = 2 * CAP
STEPS = (1, 3, 2)
TARGETS = [(d, flip) for d in (0, 1, 3, 2) for flip in (0, 1)]
VMEM = pl.BlockSpec(memory_space=pltpu.VMEM)
SMEM = pl.BlockSpec(memory_space=pltpu.SMEM)
ANY = pl.BlockSpec(memory_space=pl.ANY)
HBM = pl.BlockSpec(memory_space=pltpu.HBM)


def place(x, y, core):
    return ((x % SIDE) * SIDE + y % SIDE) * 2 + core % 2


def routes_of(step):
    return [
        (place(x, y, core), place(*step(x, y, core)))
        for x in range(SIDE)
        for y in range(SIDE)
        for core in range(2)
    ]


def gather_route(d):
    return routes_of(lambda x, y, core: (x + d, y, core) if core == 0 else (x, y + d, core))


def slot_route(d, flip):
    return routes_of(
        lambda x, y, core: (x, y + d, core + flip) if core == 0 else (x + d, y, core + flip)
    )


def back(route):
    return [(b, a) for a, b in route]


def target_experts():
    me = lax.axis_index("expert")
    x, y, core = me // (2 * SIDE), (me // 2) % SIDE, me % 2
    ids = [
        jnp.where(core == 0, place(x, y + d, core + flip), place(x + d, y, core + flip))
        for d, flip in TARGETS
    ]
    return jnp.stack(ids).astype(jnp.int32)


def call(kernel, name, out_shape, args, scratch=(), after=(), flops=1 << 20):
    one = not isinstance(out_shape, list)
    count = 1 if one else len(out_shape)
    n = len(args)

    def body(*refs):
        kernel(*refs[:n], *refs[n + len(after) :])

    return pl.pallas_call(
        body,
        out_shape=out_shape,
        in_specs=[SMEM if a.dtype == jnp.int32 and a.ndim == 1 else VMEM for a in args]
        + [ANY] * len(after),
        out_specs=VMEM if one else [VMEM] * count,
        scratch_shapes=list(scratch),
        compiler_params=pltpu.CompilerParams(vmem_limit_bytes=16 << 20),
        cost_estimate=pl.CostEstimate(flops=flops, bytes_accessed=0, transcendentals=0),
        name=name,
    )(*args, *after)


def bf16(*shape):
    return jax.ShapeDtypeStruct(shape, jnp.bfloat16)


def f32(*shape):
    return jax.ShapeDtypeStruct(shape, jnp.float32)


def pack_kernel(own, routes, gates, packed, named, gated, sems):
    copies = [
        pltpu.make_async_copy(routes, named, sems.at[0]),
        pltpu.make_async_copy(gates, gated, sems.at[1]),
        pltpu.make_async_copy(own, packed.at[:, 0:D], sems.at[2]),
    ]
    for copy in copies:
        copy.start()
    packed[2 * TOP :, D:] = jnp.zeros((TOK - 2 * TOP, TOK), jnp.bfloat16)
    copies[0].wait()
    copies[1].wait()
    both = jnp.concatenate([named[...].astype(jnp.float32), gated[...]], axis=0)
    packed[0 : 2 * TOP, D:] = both.astype(jnp.bfloat16)
    copies[2].wait()


def slots_kernel(ids, *refs):
    blocks, (spread, slots) = refs[0:4], refs[4:]
    expert = lax.broadcasted_iota(jnp.int32, (EXPERTS, TOK), 0).astype(jnp.float32)
    earlier = lax.broadcasted_iota(jnp.int32, (TOK, TOK), 0) < lax.broadcasted_iota(
        jnp.int32, (TOK, TOK), 1
    )
    earlier = jnp.where(earlier, 1.0, 0.0).astype(jnp.bfloat16)
    slot = lax.broadcasted_iota(jnp.int32, (CAP, TOK), 0).astype(jnp.float32)
    for j in range(4):
        block = blocks[j][0 : 2 * TOP, D:].astype(jnp.float32)
        named = jnp.zeros((EXPERTS, TOK), jnp.float32)
        gate = jnp.zeros((EXPERTS, TOK), jnp.float32)
        for k in range(TOP):
            hit = expert == block[k : k + 1, :]
            named = named + jnp.where(hit, 1.0, 0.0)
            gate = gate + jnp.where(hit, block[TOP + k : TOP + k + 1, :], 0.0)
        before = jnp.dot(named.astype(jnp.bfloat16), earlier, preferred_element_type=jnp.float32)
        slots[j, 0:EXPERTS, :] = jnp.where(named > 0.0, before, -1.0)
        slots[j, EXPERTS : 2 * EXPERTS, :] = gate
        for i in range(len(TARGETS)):
            hit = slot == slots[j, pl.ds(ids[i], 1), :]
            spread[j, i * CAP : (i + 1) * CAP, :] = jnp.where(hit, 1.0, 0.0)


def weights_kernel(ids, slots, weights):
    slot = lax.broadcasted_iota(jnp.int32, (CAP, TOK), 0).astype(jnp.float32)
    empty = jnp.zeros((CAP, TOK), jnp.float32)
    for pair in range(2):
        whole = []
        for i in range(len(TARGETS)):
            halves = []
            for j in (2 * pair, 2 * pair + 1):
                hit = slot == slots[j, pl.ds(ids[i], 1), :]
                halves.append(jnp.where(hit, slots[j, pl.ds(ids[i] + EXPERTS, 1), :], 0.0))
            whole.append(jnp.concatenate([halves[0], empty], axis=1))
            whole.append(jnp.concatenate([empty, halves[1]], axis=1))
        weights[pair] = jnp.concatenate(whole, axis=0).T.astype(jnp.bfloat16)


def fill_kernel(first, spread, *refs):
    tokens, outs = refs[0:4], refs[4:]
    rows = pl.ds(first * CAP, len(outs) * CAP)
    for t in range(D // TILE):
        cut = pl.ds(t * TILE, TILE)
        made = [
            jnp.dot(
                spread[j, rows, :].astype(jnp.bfloat16),
                tokens[j][:, cut],
                preferred_element_type=jnp.float32,
            )
            for j in range(4)
        ]
        for i, out in enumerate(outs):
            out[:, cut] = jnp.concatenate(
                [m[i * CAP : (i + 1) * CAP] for m in made], axis=0
            ).astype(jnp.bfloat16)


def fill_slots(spread, tokens, first, count, after=()):
    kernel = functools.partial(fill_kernel, first)
    return call(kernel, "fill", [bf16(2 * PAIR, D)] * count, (spread, *tokens), after=after)


def expert_kernel(*refs):
    rows, (w_gate, w_up, w_down), outs, hidden = refs[:2], refs[2:5], refs[5:7], refs[7]
    for f in range(FF // TILE):
        cut = pl.ds(f * TILE, TILE)
        block = jnp.concatenate([r[...] for r in rows], axis=0)
        pre_g = jnp.dot(block, w_gate[:, cut], preferred_element_type=jnp.float32)
        pre_u = jnp.dot(block, w_up[:, cut], preferred_element_type=jnp.float32)
        hidden[:, cut] = (pre_g / (1.0 + jnp.exp(-pre_g)) * pre_u).astype(jnp.bfloat16)
    for t in range(D // (2 * TILE)):
        cut = pl.ds(t * 2 * TILE, 2 * TILE)
        done = jnp.dot(hidden[...], w_down[:, cut], preferred_element_type=jnp.float32)
        for i in range(2):
            outs[i][:, cut] = done[i * 2 * PAIR : (i + 1) * 2 * PAIR].astype(jnp.bfloat16)


def expert_forward(rows, weights, after=()):
    scratch = [pltpu.VMEM((4 * PAIR, FF), jnp.bfloat16)]
    outs = [bf16(2 * PAIR, D)] * 2
    flops = 24 * PAIR * D * FF
    return call(expert_kernel, "expert", outs, (*rows, *weights), scratch, after, flops)


def combine_kernel(part, *refs):
    weights, rows, outs, gathered = refs[0], refs[1:9], refs[9:13], refs[13]
    first, last = PARTS[part], PARTS[part + 1]
    for pair in range(2):
        for at in range(first, last, 2 * TILE):
            width = min(2 * TILE, last - at)
            for i in range(len(TARGETS)):
                gathered[i * PAIR : (i + 1) * PAIR, 0:width] = rows[i][
                    pair * PAIR : (pair + 1) * PAIR, pl.ds(at, width)
                ]
            mixed = jnp.dot(
                weights[pair], gathered[:, 0:width], preferred_element_type=jnp.float32
            )
            cut = pl.ds(at - first, width)
            outs[2 * pair][:, cut] = mixed[0:TOK].astype(jnp.bfloat16)
            outs[2 * pair + 1][:, cut] = mixed[TOK : 2 * TOK].astype(jnp.bfloat16)


def combine(weights, rows, part, after=()):
    kernel = functools.partial(combine_kernel, part)
    scratch = [pltpu.VMEM((len(TARGETS) * PAIR, 2 * TILE), jnp.bfloat16)]
    outs = [bf16(TOK, PARTS[part + 1] - PARTS[part])] * 4
    return call(kernel, "combine", outs, (weights, *rows), scratch, after)


def finish_kernel(part, own, *refs):
    blocks, out = refs[:4], refs[4]
    mixed = own[:, PARTS[part] : PARTS[part + 1]].astype(jnp.float32)
    for block in blocks:
        mixed = mixed + block[...].astype(jnp.float32)
    out[...] = mixed.astype(jnp.bfloat16)


def on_device(tokens_a, routes_a, gates_a, w_gate, w_up, w_down):
    own = tokens_a[0]
    expert = (w_gate[0, 0], w_up[0, 0], w_down[0, 0])
    ids = target_experts()

    def send(block, route):
        return lax.ppermute(block, "expert", route)

    given = (own, routes_a[0].T, gates_a[0].T)
    packed = pl.pallas_call(
        pack_kernel,
        out_shape=bf16(TOK, D + TOK),
        in_specs=[HBM] * 3,
        out_specs=VMEM,
        scratch_shapes=[
            pltpu.VMEM((TOP, TOK), jnp.int32),
            pltpu.VMEM((TOP, TOK), jnp.float32),
            pltpu.SemaphoreType.DMA((3,)),
        ],
        compiler_params=pltpu.CompilerParams(vmem_limit_bytes=16 << 20),
        name="pack",
    )(*[pltpu.with_memory_space_constraint(a, pltpu.HBM) for a in given])
    tokens = [packed] + [send(packed, gather_route(d)) for d in STEPS]
    spread, slots = call(
        slots_kernel,
        "slots",
        [f32(4, len(TARGETS) * CAP, TOK), f32(4, 2 * EXPERTS, TOK)],
        (ids, *tokens),
    )

    def out(i, block):
        return send(block, slot_route(*TARGETS[i]))

    def home(i, block):
        return send(block, back(slot_route(*TARGETS[i])))

    results = [None] * len(TARGETS)
    far_rows = fill_slots(spread, tokens, 6, 2)
    far = [out(i + 6, block) for i, block in enumerate(far_rows)]
    near_rows = fill_slots(spread, tokens, 2, 4, after=(far_rows[0],))
    near = [out(i + 2, block) for i, block in enumerate(near_rows)]
    here = list(fill_slots(spread, tokens, 0, 2))
    here[1] = out(1, here[1])
    weights = call(weights_kernel, "weights", bf16(2, 2 * TOK, len(TARGETS) * PAIR), (ids, slots))
    for n, rows in ((6, far), (4, near[2:4]), (2, near[0:2]), (0, here)):
        done = expert_forward(rows, expert)
        results[n : n + 2] = [
            block if n + i == 0 else home(n + i, block) for i, block in enumerate(done)
        ]
    count = lax.axis_size("section")
    onward = [((i - 1) % count, i) for i in range(count)]
    moved, after = [], ()
    for part in range(len(PARTS) - 1):
        partial = combine(weights, results, part, after)
        after = (partial[0],)
        arrived = [send(block, back(gather_route(d))) for d, block in zip(STEPS, partial[1:])]
        layer_a = call(
            functools.partial(finish_kernel, part),
            "finish",
            bf16(TOK, PARTS[part + 1] - PARTS[part]),
            (packed, partial[0], *arrived),
        )
        moved.append(lax.ppermute(layer_a, "section", onward))
    joined = None
    for part, block in enumerate(moved):
        joined = join(block, part, joined)
    return joined[None]


def join_kernel(part, block, *refs):
    out, sem = refs[-2:]
    copy = pltpu.make_async_copy(block, out.at[:, pl.ds(PARTS[part], PARTS[part + 1] - PARTS[part])], sem)
    copy.start()
    copy.wait()


def join(block, part, joined):
    args = (block,) if joined is None else (block, joined)
    return pl.pallas_call(
        functools.partial(join_kernel, part),
        out_shape=bf16(TOK, D),
        in_specs=[VMEM, HBM][: len(args)],
        out_specs=HBM,
        scratch_shapes=[pltpu.SemaphoreType.DMA(())],
        input_output_aliases={} if joined is None else {1: 0},
        compiler_params=pltpu.CompilerParams(vmem_limit_bytes=16 << 20),
        name="join",
    )(*args)


def solution(mesh):
    in_specs = (
        P("section", "expert", None),
        P("section", "expert", None),
        P("section", "expert", None),
        P("section", "expert", None, None),
        P("section", "expert", None, None),
        P("section", "expert", None, None),
    )
    out_specs = P("section", "expert", None)
    return jax.shard_map(
        on_device, mesh=mesh, in_specs=in_specs, out_specs=out_specs, check_vma=False
    )
```

```python
import functools

import jax
import jax.numpy as jnp
from jax import lax
from jax.experimental import pallas as pl
from jax.experimental.pallas import tpu as pltpu
from jax.sharding import PartitionSpec as P

EXPERTS = 32
CAP = 40
SIDE = 4
TOK = 128
TOP = 8
D = 2048
FF = 768
PARTS = (0, 1024, D)
TILE = 256
PAIR = 2 * CAP
STEPS = (1, 3, 2)
TARGETS = [(d, flip) for d in (0, 1, 3, 2) for flip in (0, 1)]
VMEM = pl.BlockSpec(memory_space=pltpu.VMEM)
SMEM = pl.BlockSpec(memory_space=pltpu.SMEM)
ANY = pl.BlockSpec(memory_space=pl.ANY)
HBM = pl.BlockSpec(memory_space=pltpu.HBM)


def place(x, y, core):
    return ((x % SIDE) * SIDE + y % SIDE) * 2 + core % 2


def routes_of(step):
    return [
        (place(x, y, core), place(*step(x, y, core)))
        for x in range(SIDE)
        for y in range(SIDE)
        for core in range(2)
    ]


def gather_route(d):
    return routes_of(lambda x, y, core: (x + d, y, core) if core == 0 else (x, y + d, core))


def slot_route(d, flip):
    return routes_of(
        lambda x, y, core: (x, y + d, core + flip) if core == 0 else (x + d, y, core + flip)
    )


def back(route):
    return [(b, a) for a, b in route]


def target_experts():
    me = lax.axis_index("expert")
    x, y, core = me // (2 * SIDE), (me // 2) % SIDE, me % 2
    ids = [
        jnp.where(core == 0, place(x, y + d, core + flip), place(x + d, y, core + flip))
        for d, flip in TARGETS
    ]
    return jnp.stack(ids).astype(jnp.int32)


def call(kernel, name, out_shape, args, scratch=(), after=(), flops=1 << 20):
    one = not isinstance(out_shape, list)
    count = 1 if one else len(out_shape)
    n = len(args)

    def body(*refs):
        kernel(*refs[:n], *refs[n + len(after) :])

    return pl.pallas_call(
        body,
        out_shape=out_shape,
        in_specs=[SMEM if a.dtype == jnp.int32 and a.ndim == 1 else VMEM for a in args]
        + [ANY] * len(after),
        out_specs=VMEM if one else [VMEM] * count,
        scratch_shapes=list(scratch),
        compiler_params=pltpu.CompilerParams(vmem_limit_bytes=16 << 20),
        cost_estimate=pl.CostEstimate(flops=flops, bytes_accessed=0, transcendentals=0),
        name=name,
    )(*args, *after)


def bf16(*shape):
    return jax.ShapeDtypeStruct(shape, jnp.bfloat16)


def f32(*shape):
    return jax.ShapeDtypeStruct(shape, jnp.float32)


def pack_kernel(own, routes, gates, packed, named, gated, sems):
    copies = [
        pltpu.make_async_copy(routes, named, sems.at[0]),
        pltpu.make_async_copy(gates, gated, sems.at[1]),
        pltpu.make_async_copy(own, packed.at[:, 0:D], sems.at[2]),
    ]
    for copy in copies:
        copy.start()
    packed[2 * TOP :, D:] = jnp.zeros((TOK - 2 * TOP, TOK), jnp.bfloat16)
    copies[0].wait()
    copies[1].wait()
    both = jnp.concatenate([named[...].astype(jnp.float32), gated[...]], axis=0)
    packed[0 : 2 * TOP, D:] = both.astype(jnp.bfloat16)
    copies[2].wait()


def slots_kernel(ids, *refs):
    blocks, (spread, slots) = refs[0:4], refs[4:]
    expert = lax.broadcasted_iota(jnp.int32, (EXPERTS, TOK), 0).astype(jnp.float32)
    earlier = lax.broadcasted_iota(jnp.int32, (TOK, TOK), 0) < lax.broadcasted_iota(
        jnp.int32, (TOK, TOK), 1
    )
    earlier = jnp.where(earlier, 1.0, 0.0).astype(jnp.bfloat16)
    slot = lax.broadcasted_iota(jnp.int32, (CAP, TOK), 0).astype(jnp.float32)
    for j in range(4):
        block = blocks[j][0 : 2 * TOP, D:].astype(jnp.float32)
        named = jnp.zeros((EXPERTS, TOK), jnp.float32)
        gate = jnp.zeros((EXPERTS, TOK), jnp.float32)
        for k in range(TOP):
            hit = expert == block[k : k + 1, :]
            named = named + jnp.where(hit, 1.0, 0.0)
            gate = gate + jnp.where(hit, block[TOP + k : TOP + k + 1, :], 0.0)
        before = jnp.dot(named.astype(jnp.bfloat16), earlier, preferred_element_type=jnp.float32)
        slots[j, 0:EXPERTS, :] = jnp.where(named > 0.0, before, -1.0)
        slots[j, EXPERTS : 2 * EXPERTS, :] = gate
        for i in range(len(TARGETS)):
            hit = slot == slots[j, pl.ds(ids[i], 1), :]
            spread[j, i * CAP : (i + 1) * CAP, :] = jnp.where(hit, 1.0, 0.0)


def weights_kernel(ids, slots, weights):
    slot = lax.broadcasted_iota(jnp.int32, (CAP, TOK), 0).astype(jnp.float32)
    empty = jnp.zeros((CAP, TOK), jnp.float32)
    for pair in range(2):
        whole = []
        for i in range(len(TARGETS)):
            halves = []
            for j in (2 * pair, 2 * pair + 1):
                hit = slot == slots[j, pl.ds(ids[i], 1), :]
                halves.append(jnp.where(hit, slots[j, pl.ds(ids[i] + EXPERTS, 1), :], 0.0))
            whole.append(jnp.concatenate([halves[0], empty], axis=1))
            whole.append(jnp.concatenate([empty, halves[1]], axis=1))
        weights[pair] = jnp.concatenate(whole, axis=0).T.astype(jnp.bfloat16)


def fill_kernel(first, spread, *refs):
    tokens, outs = refs[0:4], refs[4:]
    rows = pl.ds(first * CAP, len(outs) * CAP)
    for t in range(D // TILE):
        cut = pl.ds(t * TILE, TILE)
        made = [
            jnp.dot(
                spread[j, rows, :].astype(jnp.bfloat16),
                tokens[j][:, cut],
                preferred_element_type=jnp.float32,
            )
            for j in range(4)
        ]
        for i, out in enumerate(outs):
            out[:, cut] = jnp.concatenate(
                [m[i * CAP : (i + 1) * CAP] for m in made], axis=0
            ).astype(jnp.bfloat16)


def fill_slots(spread, tokens, first, count, after=()):
    kernel = functools.partial(fill_kernel, first)
    return call(kernel, "fill", [bf16(2 * PAIR, D)] * count, (spread, *tokens), after=after)


def expert_kernel(*refs):
    rows, (w_gate, w_up, w_down), outs, hidden = refs[:2], refs[2:5], refs[5:7], refs[7]
    for f in range(FF // TILE):
        cut = pl.ds(f * TILE, TILE)
        block = jnp.concatenate([r[...] for r in rows], axis=0)
        pre_g = jnp.dot(block, w_gate[:, cut], preferred_element_type=jnp.float32)
        pre_u = jnp.dot(block, w_up[:, cut], preferred_element_type=jnp.float32)
        hidden[:, cut] = (pre_g / (1.0 + jnp.exp(-pre_g)) * pre_u).astype(jnp.bfloat16)
    for t in range(D // (2 * TILE)):
        cut = pl.ds(t * 2 * TILE, 2 * TILE)
        done = jnp.dot(hidden[...], w_down[:, cut], preferred_element_type=jnp.float32)
        for i in range(2):
            outs[i][:, cut] = done[i * 2 * PAIR : (i + 1) * 2 * PAIR].astype(jnp.bfloat16)


def expert_forward(rows, weights, after=()):
    scratch = [pltpu.VMEM((4 * PAIR, FF), jnp.bfloat16)]
    outs = [bf16(2 * PAIR, D)] * 2
    flops = 24 * PAIR * D * FF
    return call(expert_kernel, "expert", outs, (*rows, *weights), scratch, after, flops)


def combine_kernel(part, *refs):
    weights, rows, outs, gathered = refs[0], refs[1:9], refs[9:13], refs[13]
    first, last = PARTS[part], PARTS[part + 1]
    for pair in range(2):
        for at in range(first, last, 2 * TILE):
            width = min(2 * TILE, last - at)
            for i in range(len(TARGETS)):
                gathered[i * PAIR : (i + 1) * PAIR, 0:width] = rows[i][
                    pair * PAIR : (pair + 1) * PAIR, pl.ds(at, width)
                ]
            mixed = jnp.dot(
                weights[pair], gathered[:, 0:width], preferred_element_type=jnp.float32
            )
            cut = pl.ds(at - first, width)
            outs[2 * pair][:, cut] = mixed[0:TOK].astype(jnp.bfloat16)
            outs[2 * pair + 1][:, cut] = mixed[TOK : 2 * TOK].astype(jnp.bfloat16)


def combine(weights, rows, part, after=()):
    kernel = functools.partial(combine_kernel, part)
    scratch = [pltpu.VMEM((len(TARGETS) * PAIR, 2 * TILE), jnp.bfloat16)]
    outs = [bf16(TOK, PARTS[part + 1] - PARTS[part])] * 4
    return call(kernel, "combine", outs, (weights, *rows), scratch, after, 1 << 30)


def finish_kernel(part, own, *refs):
    blocks, out = refs[:4], refs[4]
    mixed = own[:, PARTS[part] : PARTS[part + 1]].astype(jnp.float32)
    for block in blocks:
        mixed = mixed + block[...].astype(jnp.float32)
    out[...] = mixed.astype(jnp.bfloat16)


def on_device(tokens_a, routes_a, gates_a, w_gate, w_up, w_down):
    own = tokens_a[0]
    expert = (w_gate[0, 0], w_up[0, 0], w_down[0, 0])
    ids = target_experts()

    def send(block, route):
        return lax.ppermute(block, "expert", route)

    given = (own, routes_a[0].T, gates_a[0].T)
    packed = pl.pallas_call(
        pack_kernel,
        out_shape=bf16(TOK, D + TOK),
        in_specs=[HBM] * 3,
        out_specs=VMEM,
        scratch_shapes=[
            pltpu.VMEM((TOP, TOK), jnp.int32),
            pltpu.VMEM((TOP, TOK), jnp.float32),
            pltpu.SemaphoreType.DMA((3,)),
        ],
        compiler_params=pltpu.CompilerParams(vmem_limit_bytes=16 << 20),
        name="pack",
    )(*[pltpu.with_memory_space_constraint(a, pltpu.HBM) for a in given])
    tokens = [packed] + [send(packed, gather_route(d)) for d in STEPS]
    spread, slots = call(
        slots_kernel,
        "slots",
        [f32(4, len(TARGETS) * CAP, TOK), f32(4, 2 * EXPERTS, TOK)],
        (ids, *tokens),
    )

    def out(i, block):
        return send(block, slot_route(*TARGETS[i]))

    def home(i, block):
        return send(block, back(slot_route(*TARGETS[i])))

    results = [None] * len(TARGETS)
    far_rows = fill_slots(spread, tokens, 6, 2)
    far = [out(i + 6, block) for i, block in enumerate(far_rows)]
    near_rows = fill_slots(spread, tokens, 2, 4, after=(far_rows[0],))
    near = [out(i + 2, block) for i, block in enumerate(near_rows)]
    here = list(fill_slots(spread, tokens, 0, 2))
    here[1] = out(1, here[1])
    weights = call(weights_kernel, "weights", bf16(2, 2 * TOK, len(TARGETS) * PAIR), (ids, slots))
    for n, rows in ((6, far), (4, near[2:4]), (2, near[0:2]), (0, here)):
        done = expert_forward(rows, expert)
        results[n : n + 2] = [
            block if n + i == 0 else home(n + i, block) for i, block in enumerate(done)
        ]
    count = lax.axis_size("section")
    onward = [((i - 1) % count, i) for i in range(count)]
    moved, after = [], ()
    for part in range(len(PARTS) - 1):
        partial = combine(weights, results, part, after)
        after = (partial[0],)
        arrived = [send(block, back(gather_route(d))) for d, block in zip(STEPS, partial[1:])]
        layer_a = call(
            functools.partial(finish_kernel, part),
            "finish",
            bf16(TOK, PARTS[part + 1] - PARTS[part]),
            (packed, partial[0], *arrived),
        )
        moved.append(lax.ppermute(layer_a, "section", onward))
    joined = None
    for part, block in enumerate(moved):
        joined = join(block, part, joined)
    return joined[None]


def join_kernel(part, block, *refs):
    out, sem = refs[-2:]
    copy = pltpu.make_async_copy(block, out.at[:, pl.ds(PARTS[part], PARTS[part + 1] - PARTS[part])], sem)
    copy.start()
    copy.wait()


def join(block, part, joined):
    args = (block,) if joined is None else (block, joined)
    return pl.pallas_call(
        functools.partial(join_kernel, part),
        out_shape=bf16(TOK, D),
        in_specs=[VMEM, HBM][: len(args)],
        out_specs=HBM,
        scratch_shapes=[pltpu.SemaphoreType.DMA(())],
        input_output_aliases={} if joined is None else {1: 0},
        compiler_params=pltpu.CompilerParams(vmem_limit_bytes=16 << 20),
        name="join",
    )(*args)


def solution(mesh):
    in_specs = (
        P("section", "expert", None),
        P("section", "expert", None),
        P("section", "expert", None),
        P("section", "expert", None, None),
        P("section", "expert", None, None),
        P("section", "expert", None, None),
    )
    out_specs = P("section", "expert", None)
    return jax.shard_map(
        on_device, mesh=mesh, in_specs=in_specs, out_specs=out_specs, check_vma=False
    )
```
